256 devices in a mesh: ctx: 32 (over y_lo, z, core), rep: 8 (over x, y_hi).
Axes of the slice: x: 4, y: 4 (y_hi: 2, y_lo: 2; y = y_hi * 2 + y_lo), z: 8, core: 2. Of those that a mesh axis runs over, the one named last changes fastest.
Arguments:
- q_policy: bfloat16 [32768, 2560], P(('rep', 'ctx')), parts along dimension 0, may hold values from -8 to 8
- kv_policy: bfloat16 [32768, 1024], P(('rep', 'ctx')), parts along dimension 0, may hold values from -8 to 8
- q_ref: bfloat16 [32768, 2560], P(('rep', 'ctx')), parts along dimension 0, may hold values from -8 to 8
- kv_ref: bfloat16 [32768, 1024], P(('rep', 'ctx')), parts along dimension 0, may hold values from -8 to 8
- doc_lengths: int32 [64], P('rep'), parts along dimension 0, may hold values from 1 to 2048, 4096 in all
- span_order: int32 [256], P('rep'), parts along dimension 0, may hold values from 0 to 31, each once
Outputs:
- attn_policy: bfloat16 [32768, 2560], P(('rep', 'ctx')), parts along dimension 0
- attn_ref: bfloat16 [32768, 2560], P(('rep', 'ctx')), parts along dimension 0
The draws below stay inside these ranges and needn't reach their ends.
There are 8 independent parts, one for each index of `rep`. The reference program is written for one: setup_inputs(seed, part) draws one part's arguments, and reference() takes and returns one part's arrays. A program takes and returns all parts, laid end to end along the dimension named above; each array names one. Nothing has to cross between parts.
Inputs may be any that keep to these rules, and one draw needn't show every extreme that they name: `doc_lengths`: the lengths of the rollout's documents in order; they sum to 4096 and the longest has 2048 tokens. Stored block i of 128 rows holds positions span_order[i] * 128 onward in order; every block of positions once.
All inputs are finite; a program needn't handle non-finite values.
Results may differ from the reference program's by a relative error of at most 0.0065.
Values may be sent and summed in bfloat16 or wider, within the bound.
A program may use at most 192 MiB of HBM per device.

```python
import math
import jax
import jax.numpy as jnp
import numpy as np
from jax import lax

HQ = 20
HK = 4
HD = 128
TOK_DEV = 128
NDOC = 8
TOKENS = 4096
LONGEST = 2048
N_CTX = 32


def build_pair(key, which):
    base = jax.random.fold_in(key, 101 + which)
    key_q, key_k, key_v = jax.random.split(base, 3)
    group_size = HQ // HK
    shape_q = (TOKENS, HK, group_size, HD)
    shape_k = (TOKENS, HK, HD)
    queries = jnp.clip(jax.random.normal(key_q, shape_q, jnp.float32), -4.0, 4.0)
    key_rows = jnp.clip(jax.random.normal(key_k, shape_k, jnp.float32), -4.0, 4.0)
    value_rows = jnp.clip(jax.random.normal(key_v, shape_k, jnp.float32), -4.0, 4.0)
    both = jnp.concatenate([key_rows.reshape(TOKENS, HK * HD), value_rows.reshape(TOKENS, HK * HD)], axis=1)
    return (queries.reshape(TOKENS, HQ * HD), both)


def draw_q_policy(key, part):
    return build_pair(key, 0)[0].astype(jnp.bfloat16)


def draw_kv_policy(key, part):
    return build_pair(key, 0)[1].astype(jnp.bfloat16)


def draw_q_ref(key, part):
    return build_pair(key, 1)[0].astype(jnp.bfloat16)


def draw_kv_ref(key, part):
    return build_pair(key, 1)[1].astype(jnp.bfloat16)


def profile(count, total, most, skew):
    loads = [(1 << 20) // math.isqrt(grade ** skew) + 1 for grade in range(2, count + 1)]
    spare, holding = total - most - (count - 1), [1] * (count - 1)
    while spare > 0:
        free = [i for i in range(count - 1) if holding[i] < most]
        mass, left = sum([loads[i] for i in free]), spare
        for i in free:
            more = min(most - holding[i], max(1, left * loads[i] // mass), spare)
            holding[i] = holding[i] + more
            spare = spare - more
    return np.array([most] + holding)


def ragged(stream_key, count, total, limit, skew):
    if count == 2:
        one = jax.random.randint(stream_key, (), max(1, total - limit), min(limit, total - 1) + 1)
        return jnp.stack([one, total - one])
    lengths = jnp.asarray(profile(count, total, limit, skew), jnp.int32)
    couples = (count - 1) // 2
    source_of, receiver = lengths[1:1 + 2 * couples:2], lengths[2:2 + 2 * couples:2]
    slack = jnp.minimum(source_of - 1, limit - receiver)
    passed = jax.random.randint(jax.random.fold_in(stream_key, 1), (couples,), 0, 1 << 20) % (slack + 1)
    lengths = lengths.at[1:1 + 2 * couples:2].set(source_of - passed).at[2:2 + 2 * couples:2].set(receiver + passed)
    return lengths[jax.random.permutation(jax.random.fold_in(stream_key, 2), count)]


def setup_inputs(seed: int = 0, part: int = 0) -> dict:
    splits = jax.random.split(jax.random.key(seed), 7)
    own_keys = jax.random.split(jax.random.fold_in(splits[6], part), 7)
    q_policy = draw_q_policy(jax.random.fold_in(jax.random.fold_in(splits[6], part), 71), part)
    kv_policy = draw_kv_policy(jax.random.fold_in(jax.random.fold_in(splits[6], part), 71), part)
    q_ref = draw_q_ref(jax.random.fold_in(jax.random.fold_in(splits[6], part), 71), part)
    kv_ref = draw_kv_ref(jax.random.fold_in(jax.random.fold_in(splits[6], part), 71), part)
    doc_lengths = ragged(own_keys[4], NDOC, TOKENS, LONGEST, 2).astype(jnp.int32)
    span_order = jax.random.permutation(own_keys[5], N_CTX).astype(jnp.int32)
    return {"q_policy": q_policy, "kv_policy": kv_policy, "q_ref": q_ref, "kv_ref": kv_ref, "doc_lengths": doc_lengths, "span_order": span_order}


def attend_model(queries, kv_rows, positions, documents):
    group_size = HQ // HK
    key_rows = kv_rows[:, :HK * HD].reshape(TOKENS, HK, HD).astype(jnp.float32)
    value_rows = kv_rows[:, HK * HD:].reshape(TOKENS, HK, HD).astype(jnp.float32)
    q_blocks = queries.reshape(TOKENS // TOK_DEV, TOK_DEV, HK, group_size, HD)
    p_blocks = positions.reshape(TOKENS // TOK_DEV, TOK_DEV)
    d_blocks = documents.reshape(TOKENS // TOK_DEV, TOK_DEV)
    score_scale = 1.0 / jnp.sqrt(jnp.float32(HD))

    def one_block(packed):
        q_block, q_pos, q_doc = packed
        scores = jnp.einsum('tkgd,skd->kgts', q_block.astype(jnp.float32), key_rows) * score_scale
        allowed = (positions[None, :] <= q_pos[:, None]) & (documents[None, :] == q_doc[:, None])
        peaks = lax.optimization_barrier(jnp.max(jnp.where(allowed, scores, -jnp.inf), axis=-1))
        weights = jnp.where(allowed, jnp.exp(scores - peaks[..., None]), 0.0)
        denominators = lax.optimization_barrier(jnp.sum(weights, axis=-1))
        rounded = lax.optimization_barrier(weights.astype(jnp.bfloat16)).astype(jnp.float32)
        summed = jnp.einsum('kgts,skd->tkgd', rounded, value_rows)
        result = summed / jnp.transpose(denominators, (2, 0, 1))[..., None]
        return result.astype(jnp.bfloat16).reshape(TOK_DEV, HQ * HD)
    outputs = lax.map(one_block, (q_blocks, p_blocks, d_blocks))
    return outputs.reshape(TOKENS, HQ * HD)

def reference(q_policy, kv_policy, q_ref, kv_ref, doc_lengths, span_order):
    rows_all = jnp.arange(TOKENS, dtype=jnp.int32)
    positions = (span_order[rows_all // TOK_DEV].astype(jnp.int32) * TOK_DEV + rows_all % TOK_DEV).astype(jnp.int32)
    doc_ends = jnp.cumsum(doc_lengths).astype(jnp.int32)
    documents = lax.optimization_barrier(jnp.sum((doc_ends[None, :] <= positions[:, None]).astype(jnp.int32), axis=1)).astype(jnp.int32)
    attn_policy = attend_model(q_policy, kv_policy, positions, documents)
    attn_ref = attend_model(q_ref, kv_ref, positions, documents)
    return (attn_policy, attn_ref)
```

```python
import functools
import math

import jax
import jax.numpy as jnp
from jax import lax
from jax.experimental import pallas as pl
from jax.experimental.pallas import tpu as pltpu
from jax.sharding import PartitionSpec as P

HK, GROUP, HD, TOK = 4, 5, 128, 128
NZ, NBLK, SPAN = 8, 32, 17
ROWS, KEYS = GROUP * TOK, SPAN * TOK
NDOC = 8
SCALE = math.log2(math.e) / math.sqrt(HD)
BIG = 131072.0
NSIG = 2 * HK
BF, F32 = jnp.bfloat16, jnp.float32
PROLOGUE = (0, 10, 20, 30, 1, 11, 21, 31, 2, 12, 22, 32, 3, 40, 13, 23, 50, 33, 4, 60)
BEFORE_S = {1: (41, 14, 24), 2: (51, 70, 34), 3: (42,), 4: (71, 62, 43, 53, 72, 63, 44, 54), 6: (74,)}
BEFORE_P = {2: (61,), 3: (52,), 4: (73, 64)}


def kernel(n_ctx, qp_ref, kvp_ref, qr_ref, kvr_ref, doc_ref, span_ref, o_ref, *scratch):
    kvb = scratch[:NSIG]
    (qbuf, kaug, vaug, pbuf, qa, abias, elog, obuf, inv,
     lk, lq, yr, ys, yqr, yqs, zr, zs, cr, cs, orecv, osend, olocal) = scratch[NSIG:]
    me = lax.axis_index("ctx")
    y, z, c = me // (2 * NZ), (me // 2) % NZ, me % 2

    def dev(yy, zz, cc):
        return {"ctx": (yy * NZ + zz) * 2 + cc}

    mesh_id = pl.DeviceIdType.MESH
    peer_y, peer_c = dev(1 - y, z, c), dev(y, z, 1 - c)
    up, down = dev(y, (z + 1) % NZ, c), dev(y, (z + NZ - 1) % NZ, c)

    def remote(src, dst, ssem, rsem, to):
        return pltpu.make_async_remote_copy(
            src_ref=src, dst_ref=dst, send_sem=ssem, recv_sem=rsem, device_id=to, device_id_type=mesh_id)

    def slot(zz):
        return c * 2 * NZ + zz * 2

    barrier = pltpu.get_barrier_semaphore()
    for to in (peer_y, peer_c, up, down):
        pl.semaphore_signal(barrier, inc=1, device_id=to, device_id_type=mesh_id)

    def kv_cols(sig):
        return pl.ds((sig % 2) * HK * HD + (sig // 2) * HD, HD)

    def local_copies(kv_ref, q_ref):
        for sig in range(NSIG):
            pltpu.make_async_copy(kv_ref.at[:, kv_cols(sig)], kvb[sig].at[slot(z) + y], lk.at[sig]).start()
        pltpu.make_async_copy(q_ref, qbuf.at[1], lq).start()

    def peer_copies(kv_ref, q_ref):
        for sig in range(NSIG):
            remote(kv_ref.at[:, kv_cols(sig)], kvb[sig].at[slot(z) + y], ys, yr.at[sig], peer_y).start()
        for j in range(HK):
            cols = pl.ds(j * GROUP * HD, GROUP * HD)
            remote(q_ref.at[:, cols], qbuf.at[0, :, cols], yqs, yqr.at[j], peer_y).start()

    @pl.when(y == 0)
    def _():
        local_copies(kvp_ref, qp_ref)

    @pl.when(y == 1)
    def _():
        local_copies(kvr_ref, qr_ref)

    pl.semaphore_wait(barrier, 4)

    @pl.when(y == 0)
    def _():
        peer_copies(kvr_ref, qr_ref)

    @pl.when(y == 1)
    def _():
        peer_copies(kvp_ref, qp_ref)

    def tick(sig, d):
        buf = kvb[sig]

        def push(view):
            remote(view, view, cs.at[sig], cr.at[sig], peer_c).start()

        if d == 0:
            mine = buf.at[slot(z) + y]
            pltpu.make_async_copy(mine, mine, lk.at[sig]).wait()
            theirs = buf.at[slot(z) + 1 - y]
            remote(theirs, theirs, ys, yr.at[sig], peer_y).wait_recv()
            view = buf.at[pl.ds(slot(z), 2)]
            for way, to in ((0, up), (1, down)):
                remote(view, view, zs.at[sig], zr.at[sig, 0, way], to).start()
            push(view)
            return
        for way, to in ((0, up), (1, down)):
            first = slot((z + NZ - d) % NZ if way == 0 else (z + d) % NZ)
            view = buf.at[pl.ds(first, 2)] if d < 4 else buf.at[pl.ds(first + way, 1)]
            remote(view, view, zs.at[sig], zr.at[sig, d - 1, way], to).wait_recv()
            if d < 4:
                onward = view if d < 3 else buf.at[pl.ds(first + way, 1)]
                remote(onward, onward, zs.at[sig], zr.at[sig, d, way], to).start()
                push(view)
        if d == 4:
            push(buf.at[pl.ds(slot((z + 4) % NZ), 2)])

    def tables():
        def fill(k, _):
            acc = jnp.int32(0)
            for m in range(NBLK):
                at = ((m // 2) % NZ) * 2 + (m % 2) * 2 * NZ + m // (2 * NZ)
                acc = jnp.where(span_ref[m] == k, jnp.int32(at), acc)
            inv[k] = acc
            return 0

        lax.fori_loop(0, NBLK, fill, 0)
        lane = lax.broadcasted_iota(jnp.int32, (TOK, HD), 1)
        row = lax.broadcasted_iota(jnp.int32, (TOK, HD), 0)
        first = jnp.where(lane == NDOC, -1000000, 0)
        last = jnp.where(lane == NDOC, 0, -1000000)
        end = jnp.int32(0)
        for k in range(NDOC):
            begin = end
            end = end + doc_ref[k]
            first = jnp.where(lane == k, begin, first)
            last = jnp.where(lane == k, end, last)

        def block(r, _):
            pos = row + (r - 16) * TOK
            hit = (pos >= first) & (pos < last)
            elog[r] = jnp.where(hit, 1.0, 0.0).astype(BF)
            return 0

        lax.fori_loop(0, NBLK + 16, block, 0)
        vaug[:, HD:] = jnp.ones((KEYS, HD), BF)
        for b in range(2):
            place = place_of(b)
            for t in range(SPAN):
                kaug[b, t * TOK:(t + 1) * TOK, HD:] = elog[place + t]
            abias[b] = ((elog[place + 16].astype(F32) - 1.0) * BIG).astype(BF)

    def place_of(b):
        source = jnp.where(b == 0, 1 - y, y) * 2 * NZ + z * 2 + c
        return span_ref[source]

    for count, item in enumerate(PROLOGUE):
        if count == 3:
            tables()
        tick(item // 10, item % 10)
    pltpu.make_async_copy(qbuf.at[1], qbuf.at[1], lq).wait()

    def scores(i):
        j, b = i // 2, i % 2
        place = place_of(b)
        for jj in range(HK):
            sig = 2 * jj

            @pl.when(j == jj)
            def _(sig=sig, jj=jj):
                @pl.when(b == 0)
                def _():
                    half = kvb[sig].at[pl.ds((1 - c) * 2 * NZ, 2 * NZ)]
                    remote(half, half, cs.at[sig], cr.at[sig], peer_c).wait_recv()
                    cols = pl.ds(jj * GROUP * HD, GROUP * HD)
                    part = qbuf.at[0, :, cols]
                    remote(part, part, yqs, yqr.at[jj], peer_y).wait_recv()

                for t in range(SPAN):
                    at = inv[jnp.maximum(place - 16 + t, 0)]
                    kaug[b, t * TOK:(t + 1) * TOK, :HD] = kvb[sig][at]

        for g in range(GROUP):
            cols = pl.ds(pl.multiple_of((j * GROUP + g) * HD, HD), HD)
            qa[g * TOK:(g + 1) * TOK, :HD] = qbuf[b, :, cols]
            qa[g * TOK:(g + 1) * TOK, HD:] = abias[b]
        s = lax.dot_general(qa[...], kaug[b], (((1,), (1,)), ((), ())), preferred_element_type=F32)
        causal = lax.broadcasted_iota(jnp.int32, (TOK, TOK), 1) <= lax.broadcasted_iota(jnp.int32, (TOK, TOK), 0)
        keep = i % 3
        for g in range(GROUP):
            sg = s[g * TOK:(g + 1) * TOK]
            diag = jnp.where(causal, sg[:, KEYS - TOK:], -BIG)
            peak = diag
            for t in range(SPAN - 1):
                peak = jnp.maximum(peak, sg[:, t * TOK:(t + 1) * TOK])
            peak = jnp.max(peak, axis=1, keepdims=True) * SCALE
            pbuf[keep, g * TOK:(g + 1) * TOK, :KEYS - TOK] = jnp.exp2(sg[:, :KEYS - TOK] * SCALE - peak).astype(BF)
            pbuf[keep, g * TOK:(g + 1) * TOK, KEYS - TOK:] = jnp.exp2(diag * SCALE - peak).astype(BF)

    def values(i):
        j, b = i // 2, i % 2
        place = place_of(b)
        for jj in range(HK):
            sig = 2 * jj + 1

            @pl.when(j == jj)
            def _(sig=sig):
                @pl.when(b == 0)
                def _():
                    half = kvb[sig].at[pl.ds((1 - c) * 2 * NZ, 2 * NZ)]
                    remote(half, half, cs.at[sig], cr.at[sig], peer_c).wait_recv()

                for t in range(SPAN):
                    at = inv[jnp.maximum(place - 16 + t, 0)]
                    vaug[t * TOK:(t + 1) * TOK, :HD] = kvb[sig][at]

        o = lax.dot_general(pbuf[i % 3], vaug[...], (((1,), (0,)), ((), ())), preferred_element_type=F32)
        o = (o[:, :HD] / o[:, HD:]).astype(BF)
        for g in range(GROUP):
            obuf[i, :, g * HD:(g + 1) * HD] = o[g * TOK:(g + 1) * TOK]
        cols = pl.ds(pl.multiple_of(j * GROUP * HD, GROUP * HD), GROUP * HD)

        @pl.when(b == 0)
        def _():
            remote(obuf.at[i], o_ref.at[y, :, cols], osend, orecv.at[j], peer_y).start()

        @pl.when(b == 1)
        def _():
            pltpu.make_async_copy(obuf.at[i], o_ref.at[y, :, cols], olocal.at[j]).start()

    @pl.loop(0, 10)
    def _(i):
        for k, items in BEFORE_S.items():
            if items:
                @pl.when(i == k)
                def _(items=items):
                    for item in items:
                        tick(item // 10, item % 10)

        @pl.when(i < 8)
        def _():
            scores(i)

        for k, items in BEFORE_P.items():
            if items:
                @pl.when(i == k)
                def _(items=items):
                    for item in items:
                        tick(item // 10, item % 10)

        @pl.when(i >= 2)
        def _():
            values(i - 2)

    for j in range(HK):
        cols = pl.ds(j * GROUP * HD, GROUP * HD)
        part = o_ref.at[1 - y, :, cols]
        remote(part, part, osend, orecv.at[j], peer_y).wait_recv()
        part = o_ref.at[y, :, cols]
        pltpu.make_async_copy(part, part, olocal.at[j]).wait()
    four = obuf.at[pl.ds(0, HK)]
    remote(four, four, osend, orecv.at[0], peer_y).wait_send()
    remote(qbuf.at[0], qbuf.at[0], yqs, yqr.at[0], peer_y).wait_send()
    eight = kvb[0].at[pl.ds(0, NSIG)]
    remote(eight, eight, ys, yr.at[0], peer_y).wait_send()
    for sig in range(NSIG):
        sent = kvb[sig].at[pl.ds(0, 14)]
        remote(sent, sent, zs.at[sig], zr.at[sig, 0, 0], up).wait_send()
        sent = kvb[sig].at[pl.ds(0, 16)]
        remote(sent, sent, cs.at[sig], cr.at[sig], peer_c).wait_send()


def on_device(n_ctx, q_policy, kv_policy, q_ref, kv_ref, doc_lengths, span_order):
    any_spec = pl.BlockSpec(memory_space=pl.ANY)
    smem = pl.BlockSpec(memory_space=pltpu.SMEM)
    dma = pltpu.SemaphoreType.DMA
    out = pl.pallas_call(
        functools.partial(kernel, n_ctx),
        out_shape=jax.ShapeDtypeStruct((2, TOK, HK * GROUP * HD), BF),
        in_specs=[any_spec] * 4 + [smem] * 2,
        out_specs=any_spec,
        scratch_shapes=[pltpu.VMEM((NBLK, TOK, HD), BF)] * NSIG
        + [
            pltpu.VMEM((2, TOK, HK * GROUP * HD), BF),
            pltpu.VMEM((2, KEYS, 2 * HD), BF),
            pltpu.VMEM((KEYS, 2 * HD), BF),
            pltpu.VMEM((3, ROWS, KEYS), BF),
            pltpu.VMEM((ROWS, 2 * HD), BF),
            pltpu.VMEM((2, TOK, HD), BF),
            pltpu.VMEM((NBLK + 16, TOK, HD), BF),
            pltpu.VMEM((2 * HK, TOK, GROUP * HD), BF),
            pltpu.SMEM((NBLK,), jnp.int32),
            dma((NSIG,)), dma, dma((NSIG,)), dma, dma((HK,)), dma,
            dma((NSIG, 4, 2)), dma((NSIG,)), dma((NSIG,)), dma((NSIG,)),
            dma((HK,)), dma, dma((HK,)),
        ],
        compiler_params=pltpu.CompilerParams(
            collective_id=0, has_side_effects=True, vmem_limit_bytes=52 * 2**20),
        cost_estimate=pl.CostEstimate(flops=6_000_000_000, bytes_accessed=4_000_000, transcendentals=12_000_000),
    )(q_policy, kv_policy, q_ref, kv_ref, doc_lengths, span_order)
    return out[0], out[1]


def solution(mesh):
    spec = P(("rep", "ctx"), None)
    return jax.shard_map(
        functools.partial(on_device, mesh.shape["ctx"]), mesh=mesh,
        in_specs=(spec, spec, spec, spec, P("rep"), P("rep")), out_specs=(spec, spec), check_vma=False)
```

```python
import functools
import math

import jax
import jax.numpy as jnp
from jax import lax
from jax.experimental import pallas as pl
from jax.experimental.pallas import tpu as pltpu
from jax.sharding import PartitionSpec as P

HK, GROUP, HD, TOK = 4, 5, 128, 128
NZ, NBLK, SPAN = 8, 32, 17
ROWS, KEYS = GROUP * TOK, SPAN * TOK
NDOC = 8
SCALE = math.log2(math.e) / math.sqrt(HD)
BIG = 131072.0
NSIG = 2 * HK
BF, F32 = jnp.bfloat16, jnp.float32
PROLOGUE = (0, 20, 10, 40, 1, 21, 30, 11, 2, 22, 41, 12, 3, 23, 31, 60, 42, 13, 4, 50, 70, 24)
BEFORE_S = {1: (32,), 2: (61, 14), 3: (71,), 4: (52,), 5: (53,), 6: (54,), 7: (74,)}
BEFORE_P = {2: (43, 51), 3: (33, 62, 44), 4: (72, 34, 63), 5: (73, 64)}


def kernel(n_ctx, qp_ref, kvp_ref, qr_ref, kvr_ref, doc_ref, span_ref, op_ref, or_ref, *scratch):
    kvb = scratch[:NSIG]
    (qbuf, kaug, vaug, pbuf, qa, abias, elog, obuf, inv,
     lk, lq, yr, ys, yqr, yqs, zr, zs, cr, cs, orecv, osend, olocal) = scratch[NSIG:]
    me = lax.axis_index("ctx")
    y, z, c = me // (2 * NZ), (me // 2) % NZ, me % 2

    def dev(yy, zz, cc):
        return {"ctx": (yy * NZ + zz) * 2 + cc}

    mesh_id = pl.DeviceIdType.MESH
    peer_y, peer_c = dev(1 - y, z, c), dev(y, z, 1 - c)
    up, down = dev(y, (z + 1) % NZ, c), dev(y, (z + NZ - 1) % NZ, c)

    def remote(src, dst, ssem, rsem, to):
        return pltpu.make_async_remote_copy(
            src_ref=src, dst_ref=dst, send_sem=ssem, recv_sem=rsem, device_id=to, device_id_type=mesh_id)

    def slot(zz):
        return c * 2 * NZ + zz * 2

    barrier = pltpu.get_barrier_semaphore()
    for to in (peer_y, peer_c, up, down):
        pl.semaphore_signal(barrier, inc=1, device_id=to, device_id_type=mesh_id)

    def kv_cols(sig):
        return pl.ds((sig % 2) * HK * HD + (sig // 2) * HD, HD)

    def local_copies(kv_ref, q_ref):
        for sig in range(NSIG):
            pltpu.make_async_copy(kv_ref.at[:, kv_cols(sig)], kvb[sig].at[slot(z) + y], lk.at[sig]).start()
        pltpu.make_async_copy(q_ref, qbuf.at[1], lq).start()

    def peer_copies(kv_ref, q_ref):
        for sig in range(NSIG):
            remote(kv_ref.at[:, kv_cols(sig)], kvb[sig].at[slot(z) + y], ys, yr.at[sig], peer_y).start()
        for j in range(HK):
            cols = pl.ds(j * GROUP * HD, GROUP * HD)
            remote(q_ref.at[:, cols], qbuf.at[0, :, cols], yqs, yqr.at[j], peer_y).start()

    @pl.when(y == 0)
    def _():
        local_copies(kvp_ref, qp_ref)

    @pl.when(y == 1)
    def _():
        local_copies(kvr_ref, qr_ref)

    pl.semaphore_wait(barrier, 4)

    @pl.when(y == 0)
    def _():
        peer_copies(kvr_ref, qr_ref)

    @pl.when(y == 1)
    def _():
        peer_copies(kvp_ref, qp_ref)

    def tick(sig, d):
        buf = kvb[sig]

        def push(view):
            remote(view, view, cs.at[sig], cr.at[sig], peer_c).start()

        if d == 0:
            mine = buf.at[pl.ds(slot(z) + y, 1)]
            theirs = buf.at[pl.ds(slot(z) + 1 - y, 1)]
            both = buf.at[pl.ds(slot(z), 2)]
            pltpu.make_async_copy(mine, mine, lk.at[sig]).wait()
            if sig < 2:
                for way, to in ((0, up), (1, down)):
                    remote(mine, mine, zs.at[sig], zr.at[sig, 0, way], to).start()
            remote(theirs, theirs, ys, yr.at[sig], peer_y).wait_recv()
            rest = theirs if sig < 2 else both
            for way, to in ((0, up), (1, down)):
                remote(rest, rest, zs.at[sig], zr.at[sig, 0, way], to).start()
            push(both)
            return
        for way, to in ((0, up), (1, down)):
            first = slot((z + NZ - d) % NZ if way == 0 else (z + d) % NZ)
            view = buf.at[pl.ds(first, 2)] if d < 4 else buf.at[pl.ds(first + way, 1)]
            remote(view, view, zs.at[sig], zr.at[sig, d - 1, way], to).wait_recv()
            if d < 4:
                onward = view if d < 3 else buf.at[pl.ds(first + way, 1)]
                remote(onward, onward, zs.at[sig], zr.at[sig, d, way], to).start()
                push(view)
        if d == 4:
            push(buf.at[pl.ds(slot((z + 4) % NZ), 2)])

    def tables():
        def fill(k, _):
            acc = jnp.int32(0)
            for m in range(NBLK):
                at = ((m // 2) % NZ) * 2 + (m % 2) * 2 * NZ + m // (2 * NZ)
                acc = jnp.where(span_ref[m] == k, jnp.int32(at), acc)
            inv[k] = acc
            return 0

        lax.fori_loop(0, NBLK, fill, 0)
        lane = lax.broadcasted_iota(jnp.int32, (TOK, HD), 1)
        row = lax.broadcasted_iota(jnp.int32, (TOK, HD), 0)
        first = jnp.where(lane == NDOC, -1000000, 0)
        last = jnp.where(lane == NDOC, 0, -1000000)
        end = jnp.int32(0)
        for k in range(NDOC):
            begin = end
            end = end + doc_ref[k]
            first = jnp.where(lane == k, begin, first)
            last = jnp.where(lane == k, end, last)

        def block(r, _):
            pos = row + (r - 16) * TOK
            hit = (pos >= first) & (pos < last)
            elog[r] = jnp.where(hit, 1.0, 0.0).astype(BF)
            return 0

        lax.fori_loop(0, NBLK + 16, block, 0)
        vaug[:, HD:] = jnp.ones((KEYS, HD), BF)
        for b in range(2):
            place = place_of(b)
            for t in range(SPAN):
                kaug[b, t * TOK:(t + 1) * TOK, HD:] = elog[place + t]
            abias[b] = ((elog[place + 16].astype(F32) - 1.0) * BIG).astype(BF)

    def place_of(b):
        source = jnp.where(b == 0, 1 - y, y) * 2 * NZ + z * 2 + c
        return span_ref[source]

    for count, item in enumerate(PROLOGUE):
        if count == 3:
            tables()
        tick(item // 10, item % 10)
    pltpu.make_async_copy(qbuf.at[1], qbuf.at[1], lq).wait()

    def scores(i):
        j, b = i // 2, i % 2
        place = place_of(b)
        for jj in range(HK):
            sig = 2 * jj

            @pl.when(j == jj)
            def _(sig=sig, jj=jj):
                @pl.when(b == 0)
                def _():
                    half = kvb[sig].at[pl.ds((1 - c) * 2 * NZ, 2 * NZ)]
                    remote(half, half, cs.at[sig], cr.at[sig], peer_c).wait_recv()
                    cols = pl.ds(jj * GROUP * HD, GROUP * HD)
                    part = qbuf.at[0, :, cols]
                    remote(part, part, yqs, yqr.at[jj], peer_y).wait_recv()

                for t in range(SPAN):
                    at = inv[jnp.maximum(place - 16 + t, 0)]
                    kaug[b, t * TOK:(t + 1) * TOK, :HD] = kvb[sig][at]

        for g in range(GROUP):
            cols = pl.ds(pl.multiple_of((j * GROUP + g) * HD, HD), HD)
            qa[g * TOK:(g + 1) * TOK, :HD] = qbuf[b, :, cols]
            qa[g * TOK:(g + 1) * TOK, HD:] = abias[b]
        s = lax.dot_general(qa[...], kaug[b], (((1,), (1,)), ((), ())), preferred_element_type=F32)
        causal = lax.broadcasted_iota(jnp.int32, (TOK, TOK), 1) <= lax.broadcasted_iota(jnp.int32, (TOK, TOK), 0)
        keep = i % 3
        for g in range(GROUP):
            sg = s[g * TOK:(g + 1) * TOK]
            diag = jnp.where(causal, sg[:, KEYS - TOK:], -BIG)
            peak = diag
            for t in range(SPAN - 1):
                peak = jnp.maximum(peak, sg[:, t * TOK:(t + 1) * TOK])
            peak = jnp.max(peak, axis=1, keepdims=True) * SCALE
            pbuf[keep, g * TOK:(g + 1) * TOK, :KEYS - TOK] = jnp.exp2(sg[:, :KEYS - TOK] * SCALE - peak).astype(BF)
            pbuf[keep, g * TOK:(g + 1) * TOK, KEYS - TOK:] = jnp.exp2(diag * SCALE - peak).astype(BF)

    def values(i):
        j, b = i // 2, i % 2
        place = place_of(b)
        for jj in range(HK):
            sig = 2 * jj + 1

            @pl.when(j == jj)
            def _(sig=sig):
                @pl.when(b == 0)
                def _():
                    half = kvb[sig].at[pl.ds((1 - c) * 2 * NZ, 2 * NZ)]
                    remote(half, half, cs.at[sig], cr.at[sig], peer_c).wait_recv()

                for t in range(SPAN):
                    at = inv[jnp.maximum(place - 16 + t, 0)]
                    vaug[t * TOK:(t + 1) * TOK, :HD] = kvb[sig][at]

        o = lax.dot_general(pbuf[i % 3], vaug[...], (((1,), (0,)), ((), ())), preferred_element_type=F32)
        o = (o[:, :HD] / o[:, HD:]).astype(BF)
        for g in range(GROUP):
            obuf[i, :, g * HD:(g + 1) * HD] = o[g * TOK:(g + 1) * TOK]
        cols = pl.ds(pl.multiple_of(j * GROUP * HD, GROUP * HD), GROUP * HD)

        @pl.when(b == 0)
        def _():
            for m, o_ref in enumerate((op_ref, or_ref)):
                @pl.when(y == m)
                def _(o_ref=o_ref):
                    remote(obuf.at[i], o_ref.at[:, cols], osend, orecv.at[j], peer_y).start()

        @pl.when(b == 1)
        def _():
            for m, o_ref in enumerate((op_ref, or_ref)):
                @pl.when(y == m)
                def _(o_ref=o_ref):
                    pltpu.make_async_copy(obuf.at[i], o_ref.at[:, cols], olocal.at[j]).start()

    @pl.loop(0, 10)
    def _(i):
        for k, items in BEFORE_S.items():
            if items:
                @pl.when(i == k)
                def _(items=items):
                    for item in items:
                        tick(item // 10, item % 10)

        @pl.when(i < 8)
        def _():
            scores(i)

        for k, items in BEFORE_P.items():
            if items:
                @pl.when(i == k)
                def _(items=items):
                    for item in items:
                        tick(item // 10, item % 10)

        @pl.when(i >= 2)
        def _():
            values(i - 2)

    for j in range(HK):
        part = obuf.at[j]
        remote(part, part, osend, orecv.at[j], peer_y).wait_recv()
        pltpu.make_async_copy(part, part, olocal.at[j]).wait()
    four = obuf.at[pl.ds(0, HK)]
    remote(four, four, osend, orecv.at[0], peer_y).wait_send()
    remote(qbuf.at[0], qbuf.at[0], yqs, yqr.at[0], peer_y).wait_send()
    eight = kvb[0].at[pl.ds(0, NSIG)]
    remote(eight, eight, ys, yr.at[0], peer_y).wait_send()
    for sig in range(NSIG):
        sent = kvb[sig].at[pl.ds(0, 14)]
        remote(sent, sent, zs.at[sig], zr.at[sig, 0, 0], up).wait_send()
        sent = kvb[sig].at[pl.ds(0, 16)]
        remote(sent, sent, cs.at[sig], cr.at[sig], peer_c).wait_send()


def on_device(n_ctx, q_policy, kv_policy, q_ref, kv_ref, doc_lengths, span_order):
    hbm = pl.BlockSpec(memory_space=pltpu.HBM)
    smem = pl.BlockSpec(memory_space=pltpu.SMEM)
    dma = pltpu.SemaphoreType.DMA
    out = pl.pallas_call(
        functools.partial(kernel, n_ctx),
        out_shape=[jax.ShapeDtypeStruct((TOK, HK * GROUP * HD), BF)] * 2,
        in_specs=[hbm] * 4 + [smem] * 2,
        out_specs=[hbm] * 2,
        scratch_shapes=[pltpu.VMEM((NBLK, TOK, HD), BF)] * NSIG
        + [
            pltpu.VMEM((2, TOK, HK * GROUP * HD), BF),
            pltpu.VMEM((2, KEYS, 2 * HD), BF),
            pltpu.VMEM((KEYS, 2 * HD), BF),
            pltpu.VMEM((3, ROWS, KEYS), BF),
            pltpu.VMEM((ROWS, 2 * HD), BF),
            pltpu.VMEM((2, TOK, HD), BF),
            pltpu.VMEM((NBLK + 16, TOK, HD), BF),
            pltpu.VMEM((2 * HK, TOK, GROUP * HD), BF),
            pltpu.SMEM((NBLK,), jnp.int32),
            dma((NSIG,)), dma, dma((NSIG,)), dma, dma((HK,)), dma,
            dma((NSIG, 4, 2)), dma((NSIG,)), dma((NSIG,)), dma((NSIG,)),
            dma((HK,)), dma, dma((HK,)),
        ],
        compiler_params=pltpu.CompilerParams(
            collective_id=0, has_side_effects=True, vmem_limit_bytes=63 * 2**20),
        cost_estimate=pl.CostEstimate(flops=6_000_000_000, bytes_accessed=4_000_000, transcendentals=12_000_000),
    )(q_policy, kv_policy, q_ref, kv_ref, doc_lengths, span_order)
    return tuple(out)


def solution(mesh):
    spec = P(("rep", "ctx"), None)
    return jax.shard_map(
        functools.partial(on_device, mesh.shape["ctx"]), mesh=mesh,
        in_specs=(spec, spec, spec, spec, P("rep"), P("rep")), out_specs=(spec, spec), check_vma=False)
```

```python
import functools
import math

import jax
import jax.numpy as jnp
from jax import lax
from jax.experimental import pallas as pl
from jax.experimental.pallas import tpu as pltpu
from jax.sharding import PartitionSpec as P

HK, GROUP, HD, TOK = 4, 5, 128, 128
NZ, NBLK, SPAN = 8, 32, 17
ROWS, KEYS = GROUP * TOK, SPAN * TOK
NDOC = 8
SCALE = math.log2(math.e) / math.sqrt(HD)
BIG = 131072.0
NSIG = 2 * HK
BF, F32 = jnp.bfloat16, jnp.float32
PROLOGUE = (0, 10, 20, 30, 1, 11, 21, 40, 2, 31, 12, 22, 3, 50, 13, 41, 23, 4, 60, 32)
BEFORE = {1: (51, 42, 14), 2: (70,), 3: (33, 24, 61), 4: (52,), 5: (43, 71, 34), 6: (62,), 7: (44, 53), 8: (72,), 9: (63, 54), 10: (73,), 11: (64,), 13: (74,)}


def kernel(n_ctx, qp_ref, kvp_ref, qr_ref, kvr_ref, doc_ref, span_ref, op_ref, or_ref, *scratch):
    kvb = scratch[:NSIG]
    (qbuf, kaug, vaug, pbuf, qa, abias, elog, obuf, inv,
     lk, lq, yr, ys, yqr, yqs, zr, zs, cr, cs, orecv, osend, olocal) = scratch[NSIG:]
    me = lax.axis_index("ctx")
    y, z, c = me // (2 * NZ), (me // 2) % NZ, me % 2

    def dev(yy, zz, cc):
        return {"ctx": (yy * NZ + zz) * 2 + cc}

    mesh_id = pl.DeviceIdType.MESH
    peer_y, peer_c = dev(1 - y, z, c), dev(y, z, 1 - c)
    up, down = dev(y, (z + 1) % NZ, c), dev(y, (z + NZ - 1) % NZ, c)

    def remote(src, dst, ssem, rsem, to):
        return pltpu.make_async_remote_copy(
            src_ref=src, dst_ref=dst, send_sem=ssem, recv_sem=rsem, device_id=to, device_id_type=mesh_id)

    def slot(zz):
        return c * 2 * NZ + zz * 2

    barrier = pltpu.get_barrier_semaphore()
    for to in (peer_y, peer_c, up, down):
        pl.semaphore_signal(barrier, inc=1, device_id=to, device_id_type=mesh_id)

    def kv_cols(sig):
        return pl.ds((sig % 2) * HK * HD + (sig // 2) * HD, HD)

    def local_copies(kv_ref, q_ref):
        for sig in range(NSIG):
            pltpu.make_async_copy(kv_ref.at[:, kv_cols(sig)], kvb[sig].at[slot(z) + y], lk.at[sig]).start()
        pltpu.make_async_copy(q_ref, qbuf.at[1], lq).start()

    def peer_copies(kv_ref, q_ref):
        for sig in range(NSIG):
            remote(kv_ref.at[:, kv_cols(sig)], kvb[sig].at[slot(z) + y], ys, yr.at[sig], peer_y).start()
        for j in range(HK):
            cols = pl.ds(j * GROUP * HD, GROUP * HD)
            remote(q_ref.at[:, cols], qbuf.at[0, :, cols], yqs, yqr.at[j], peer_y).start()

    @pl.when(y == 0)
    def _():
        local_copies(kvp_ref, qp_ref)

    @pl.when(y == 1)
    def _():
        local_copies(kvr_ref, qr_ref)

    pl.semaphore_wait(barrier, 4)

    @pl.when(y == 0)
    def _():
        peer_copies(kvr_ref, qr_ref)

    @pl.when(y == 1)
    def _():
        peer_copies(kvp_ref, qp_ref)

    def tick(sig, d):
        buf = kvb[sig]

        def push(view):
            remote(view, view, cs.at[sig], cr.at[sig], peer_c).start()

        if d == 0:
            mine = buf.at[pl.ds(slot(z) + y, 1)]
            theirs = buf.at[pl.ds(slot(z) + 1 - y, 1)]
            both = buf.at[pl.ds(slot(z), 2)]
            pltpu.make_async_copy(mine, mine, lk.at[sig]).wait()
            if sig < 2:
                for way, to in ((0, up), (1, down)):
                    remote(mine, mine, zs.at[sig], zr.at[sig, 0, way], to).start()
            remote(theirs, theirs, ys, yr.at[sig], peer_y).wait_recv()
            rest = theirs if sig < 2 else both
            for way, to in ((0, up), (1, down)):
                remote(rest, rest, zs.at[sig], zr.at[sig, 0, way], to).start()
            push(both)
            return
        for way, to in ((0, up), (1, down)):
            first = slot((z + NZ - d) % NZ if way == 0 else (z + d) % NZ)
            view = buf.at[pl.ds(first, 2)] if d < 4 else buf.at[pl.ds(first + way, 1)]
            remote(view, view, zs.at[sig], zr.at[sig, d - 1, way], to).wait_recv()
            if d < 4:
                onward = view if d < 3 else buf.at[pl.ds(first + way, 1)]
                remote(onward, onward, zs.at[sig], zr.at[sig, d, way], to).start()
                push(view)
        if d == 4:
            push(buf.at[pl.ds(slot((z + 4) % NZ), 2)])

    def tables():
        def fill(k, _):
            acc = jnp.int32(0)
            for m in range(NBLK):
                at = ((m // 2) % NZ) * 2 + (m % 2) * 2 * NZ + m // (2 * NZ)
                acc = jnp.where(span_ref[m] == k, jnp.int32(at), acc)
            inv[k] = acc
            return 0

        lax.fori_loop(0, NBLK, fill, 0)
        lane = lax.broadcasted_iota(jnp.int32, (TOK, HD), 1)
        row = lax.broadcasted_iota(jnp.int32, (TOK, HD), 0)
        first = jnp.where(lane == NDOC, -1000000, 0)
        last = jnp.where(lane == NDOC, 0, -1000000)
        end = jnp.int32(0)
        for k in range(NDOC):
            begin = end
            end = end + doc_ref[k]
            first = jnp.where(lane == k, begin, first)
            last = jnp.where(lane == k, end, last)

        def block(r, _):
            pos = row + (r - 16) * TOK
            hit = (pos >= first) & (pos < last)
            elog[r] = jnp.where(hit, 1.0, 0.0).astype(BF)
            return 0

        lax.fori_loop(0, NBLK + 16, block, 0)
        vaug[:, HD:] = jnp.ones((KEYS, HD), BF)
        for b in range(2):
            place = place_of(b)
            for t in range(SPAN):
                kaug[b, t * TOK:(t + 1) * TOK, HD:] = elog[place + t]
            abias[b] = ((elog[place + 16].astype(F32) - 1.0) * BIG).astype(BF)

    def place_of(b):
        source = jnp.where(b == 0, 1 - y, y) * 2 * NZ + z * 2 + c
        return span_ref[source]

    for count, item in enumerate(PROLOGUE):
        if count == 3:
            tables()
        tick(item // 10, item % 10)
    pltpu.make_async_copy(qbuf.at[1], qbuf.at[1], lq).wait()

    def scores(i):
        j, b = i // 2, i % 2
        place = place_of(b)
        for jj in range(HK):
            sig = 2 * jj

            @pl.when(j == jj)
            def _(sig=sig, jj=jj):
                @pl.when(b == 0)
                def _():
                    half = kvb[sig].at[pl.ds((1 - c) * 2 * NZ, 2 * NZ)]
                    remote(half, half, cs.at[sig], cr.at[sig], peer_c).wait_recv()
                    cols = pl.ds(jj * GROUP * HD, GROUP * HD)
                    part = qbuf.at[0, :, cols]
                    remote(part, part, yqs, yqr.at[jj], peer_y).wait_recv()

                for t in range(SPAN):
                    at = inv[jnp.maximum(place - 16 + t, 0)]
                    kaug[b, t * TOK:(t + 1) * TOK, :HD] = kvb[sig][at]

        for g in range(GROUP):
            cols = pl.ds(pl.multiple_of((j * GROUP + g) * HD, HD), HD)
            qa[g * TOK:(g + 1) * TOK, :HD] = qbuf[b, :, cols]
            qa[g * TOK:(g + 1) * TOK, HD:] = abias[b]
        s = lax.dot_general(qa[...], kaug[b], (((1,), (1,)), ((), ())), preferred_element_type=F32)
        causal = lax.broadcasted_iota(jnp.int32, (TOK, TOK), 1) <= lax.broadcasted_iota(jnp.int32, (TOK, TOK), 0)
        keep = b
        for g in range(GROUP):
            sg = s[g * TOK:(g + 1) * TOK]
            diag = jnp.where(causal, sg[:, KEYS - TOK:], -BIG)
            peak = diag
            for t in range(SPAN - 1):
                peak = jnp.maximum(peak, sg[:, t * TOK:(t + 1) * TOK])
            peak = jnp.max(peak, axis=1, keepdims=True) * SCALE
            pbuf[keep, g * TOK:(g + 1) * TOK, :KEYS - TOK] = jnp.exp2(sg[:, :KEYS - TOK] * SCALE - peak).astype(BF)
            pbuf[keep, g * TOK:(g + 1) * TOK, KEYS - TOK:] = jnp.exp2(diag * SCALE - peak).astype(BF)

    def values(i):
        j, b = i // 2, i % 2
        place = place_of(b)
        for jj in range(HK):
            sig = 2 * jj + 1

            @pl.when(j == jj)
            def _(sig=sig):
                @pl.when(b == 0)
                def _():
                    half = kvb[sig].at[pl.ds((1 - c) * 2 * NZ, 2 * NZ)]
                    remote(half, half, cs.at[sig], cr.at[sig], peer_c).wait_recv()

                for t in range(SPAN):
                    at = inv[jnp.maximum(place - 16 + t, 0)]
                    vaug[t * TOK:(t + 1) * TOK, :HD] = kvb[sig][at]

        o = lax.dot_general(pbuf[b], vaug[...], (((1,), (0,)), ((), ())), preferred_element_type=F32)
        o = (o[:, :HD] / o[:, HD:]).astype(BF)
        for g in range(GROUP):
            obuf[i, :, g * HD:(g + 1) * HD] = o[g * TOK:(g + 1) * TOK]
        cols = pl.ds(pl.multiple_of(j * GROUP * HD, GROUP * HD), GROUP * HD)

        @pl.when(b == 0)
        def _():
            for m, o_ref in enumerate((op_ref, or_ref)):
                @pl.when(y == m)
                def _(o_ref=o_ref):
                    remote(obuf.at[i], o_ref.at[:, cols], osend, orecv.at[j], peer_y).start()

        @pl.when(b == 1)
        def _():
            for m, o_ref in enumerate((op_ref, or_ref)):
                @pl.when(y == m)
                def _(o_ref=o_ref):
                    pltpu.make_async_copy(obuf.at[i], o_ref.at[:, cols], olocal.at[j]).start()

    @pl.loop(0, 4 * HK)
    def _(step):
        for k, items in BEFORE.items():
            @pl.when(step == k)
            def _(items=items):
                for item in items:
                    tick(item // 10, item % 10)

        i = step // 4 * 2 + step % 2

        @pl.when(step % 4 < 2)
        def _():
            scores(i)

        @pl.when(step % 4 >= 2)
        def _():
            values(i)

    for j in range(HK):
        part = obuf.at[j]
        remote(part, part, osend, orecv.at[j], peer_y).wait_recv()
        pltpu.make_async_copy(part, part, olocal.at[j]).wait()
    four = obuf.at[pl.ds(0, HK)]
    remote(four, four, osend, orecv.at[0], peer_y).wait_send()
    remote(qbuf.at[0], qbuf.at[0], yqs, yqr.at[0], peer_y).wait_send()
    eight = kvb[0].at[pl.ds(0, NSIG)]
    remote(eight, eight, ys, yr.at[0], peer_y).wait_send()
    for sig in range(NSIG):
        sent = kvb[sig].at[pl.ds(0, 14)]
        remote(sent, sent, zs.at[sig], zr.at[sig, 0, 0], up).wait_send()
        sent = kvb[sig].at[pl.ds(0, 16)]
        remote(sent, sent, cs.at[sig], cr.at[sig], peer_c).wait_send()


def on_device(n_ctx, q_policy, kv_policy, q_ref, kv_ref, doc_lengths, span_order):
    hbm = pl.BlockSpec(memory_space=pltpu.HBM)
    smem = pl.BlockSpec(memory_space=pltpu.SMEM)
    dma = pltpu.SemaphoreType.DMA
    out = pl.pallas_call(
        functools.partial(kernel, n_ctx),
        out_shape=[jax.ShapeDtypeStruct((TOK, HK * GROUP * HD), BF)] * 2,
        in_specs=[hbm] * 4 + [smem] * 2,
        out_specs=[hbm] * 2,
        scratch_shapes=[pltpu.VMEM((NBLK, TOK, HD), BF)] * NSIG
        + [
            pltpu.VMEM((2, TOK, HK * GROUP * HD), BF),
            pltpu.VMEM((2, KEYS, 2 * HD), BF),
            pltpu.VMEM((KEYS, 2 * HD), BF),
            pltpu.VMEM((2, ROWS, KEYS), BF),
            pltpu.VMEM((ROWS, 2 * HD), BF),
            pltpu.VMEM((2, TOK, HD), BF),
            pltpu.VMEM((NBLK + 16, TOK, HD), BF),
            pltpu.VMEM((2 * HK, TOK, GROUP * HD), BF),
            pltpu.SMEM((NBLK,), jnp.int32),
            dma((NSIG,)), dma, dma((NSIG,)), dma, dma((HK,)), dma,
            dma((NSIG, 4, 2)), dma((NSIG,)), dma((NSIG,)), dma((NSIG,)),
            dma((HK,)), dma, dma((HK,)),
        ],
        compiler_params=pltpu.CompilerParams(
            collective_id=0, has_side_effects=True, vmem_limit_bytes=63 * 2**20),
        cost_estimate=pl.CostEstimate(flops=6_000_000_000, bytes_accessed=4_000_000, transcendentals=12_000_000),
    )(q_policy, kv_policy, q_ref, kv_ref, doc_lengths, span_order)
    return tuple(out)


def solution(mesh):
    spec = P(("rep", "ctx"), None)
    return jax.shard_map(
        functools.partial(on_device, mesh.shape["ctx"]), mesh=mesh,
        in_specs=(spec, spec, spec, spec, P("rep"), P("rep")), out_specs=(spec, spec), check_vma=False)
```

```python
import functools
import math

import jax
import jax.numpy as jnp
from jax import lax
from jax.experimental import pallas as pl
from jax.experimental.pallas import tpu as pltpu
from jax.sharding import PartitionSpec as P

HK, GROUP, HD, TOK = 4, 5, 128, 128
NZ, NBLK, SPAN = 8, 32, 17
ROWS, KEYS = GROUP * TOK, SPAN * TOK
NDOC = 8
SCALE = math.log2(math.e) / math.sqrt(HD)
BIG = 131072.0
NSIG = 2 * HK
BF, F32 = jnp.bfloat16, jnp.float32
AHEAD, QUERIES_AT = 4, (4, 6, 9, 12)
PROLOGUE = (0, 10, 20, 30, 1, 11, 21, 40, 2, 31, 12, 22, 3, 50, 13, 41, 23, 4, 60, 32)
BEFORE = {1: (51, 42, 14), 2: (70,), 3: (33, 24, 61), 4: (52,), 5: (43, 71, 34), 6: (62,), 7: (44, 53), 8: (72,), 9: (63, 54), 10: (73,), 11: (64,), 13: (74,)}
OWN_ORDER = tuple(k // 10 for k in PROLOGUE + sum(BEFORE.values(), ()) if k % 10 == 0)


def kernel(n_ctx, qp_ref, kvp_ref, qr_ref, kvr_ref, doc_ref, span_ref, op_ref, or_ref, *scratch):
    kvb = scratch[:NSIG]
    (qbuf, kaug, vaug, pbuf, qa, abias, elog, obuf, inv,
     lk, lq, yr, ys, yqr, yqs, zr, zs, cr, cs, orecv, osend, olocal) = scratch[NSIG:]
    me = lax.axis_index("ctx")
    y, z, c = me // (2 * NZ), (me // 2) % NZ, me % 2

    def dev(yy, zz, cc):
        return {"ctx": (yy * NZ + zz) * 2 + cc}

    mesh_id = pl.DeviceIdType.MESH
    peer_y, peer_c = dev(1 - y, z, c), dev(y, z, 1 - c)
    up, down = dev(y, (z + 1) % NZ, c), dev(y, (z + NZ - 1) % NZ, c)

    def remote(src, dst, ssem, rsem, to):
        return pltpu.make_async_remote_copy(
            src_ref=src, dst_ref=dst, send_sem=ssem, recv_sem=rsem, device_id=to, device_id_type=mesh_id)

    def slot(zz):
        return c * 2 * NZ + zz * 2

    barrier = pltpu.get_barrier_semaphore()
    for to in (peer_y, peer_c, up, down):
        pl.semaphore_signal(barrier, inc=1, device_id=to, device_id_type=mesh_id)

    def kv_cols(sig):
        return pl.ds((sig % 2) * HK * HD + (sig // 2) * HD, HD)

    def local_copies(kv_ref, q_ref):
        for sig in range(NSIG):
            pltpu.make_async_copy(kv_ref.at[:, kv_cols(sig)], kvb[sig].at[slot(z) + y], lk.at[sig]).start()
        pltpu.make_async_copy(q_ref, qbuf.at[1], lq).start()

    def kv_send(sig):
        for m, kv_ref in enumerate((kvr_ref, kvp_ref)):
            @pl.when(y == m)
            def _(kv_ref=kv_ref):
                remote(kv_ref.at[:, kv_cols(sig)], kvb[sig].at[slot(z) + y], ys, yr.at[sig], peer_y).start()

    def q_send(j):
        cols = pl.ds(j * GROUP * HD, GROUP * HD)
        for m, q_ref in enumerate((qr_ref, qp_ref)):
            @pl.when(y == m)
            def _(q_ref=q_ref):
                remote(q_ref.at[:, cols], qbuf.at[0, :, cols], yqs, yqr.at[j], peer_y).start()

    @pl.when(y == 0)
    def _():
        local_copies(kvp_ref, qp_ref)

    @pl.when(y == 1)
    def _():
        local_copies(kvr_ref, qr_ref)

    pl.semaphore_wait(barrier, 4)

    for sig in OWN_ORDER[:AHEAD]:
        kv_send(sig)

    def tick(sig, d):
        buf = kvb[sig]

        def push(view):
            remote(view, view, cs.at[sig], cr.at[sig], peer_c).start()

        if d == 0:
            mine = buf.at[pl.ds(slot(z) + y, 1)]
            theirs = buf.at[pl.ds(slot(z) + 1 - y, 1)]
            both = buf.at[pl.ds(slot(z), 2)]
            pltpu.make_async_copy(mine, mine, lk.at[sig]).wait()
            if sig < 2:
                for way, to in ((0, up), (1, down)):
                    remote(mine, mine, zs.at[sig], zr.at[sig, 0, way], to).start()
            remote(theirs, theirs, ys, yr.at[sig], peer_y).wait_recv()
            rest = theirs if sig < 2 else both
            for way, to in ((0, up), (1, down)):
                remote(rest, rest, zs.at[sig], zr.at[sig, 0, way], to).start()
            push(both)
            return
        for way, to in ((0, up), (1, down)):
            first = slot((z + NZ - d) % NZ if way == 0 else (z + d) % NZ)
            view = buf.at[pl.ds(first, 2)] if d < 4 else buf.at[pl.ds(first + way, 1)]
            remote(view, view, zs.at[sig], zr.at[sig, d - 1, way], to).wait_recv()
            if d < 4:
                onward = view if d < 3 else buf.at[pl.ds(first + way, 1)]
                remote(onward, onward, zs.at[sig], zr.at[sig, d, way], to).start()
                push(view)
        if d == 4:
            push(buf.at[pl.ds(slot((z + 4) % NZ), 2)])

    def tables():
        def fill(k, _):
            acc = jnp.int32(0)
            for m in range(NBLK):
                at = ((m // 2) % NZ) * 2 + (m % 2) * 2 * NZ + m // (2 * NZ)
                acc = jnp.where(span_ref[m] == k, jnp.int32(at), acc)
            inv[k] = acc
            return 0

        lax.fori_loop(0, NBLK, fill, 0)
        lane = lax.broadcasted_iota(jnp.int32, (TOK, HD), 1)
        row = lax.broadcasted_iota(jnp.int32, (TOK, HD), 0)
        first = jnp.where(lane == NDOC, -1000000, 0)
        last = jnp.where(lane == NDOC, 0, -1000000)
        end = jnp.int32(0)
        for k in range(NDOC):
            begin = end
            end = end + doc_ref[k]
            first = jnp.where(lane == k, begin, first)
            last = jnp.where(lane == k, end, last)

        def block(r, _):
            pos = row + (r - 16) * TOK
            hit = (pos >= first) & (pos < last)
            elog[r] = jnp.where(hit, 1.0, 0.0).astype(BF)
            return 0

        lax.fori_loop(0, NBLK + 16, block, 0)
        vaug[:, HD:] = jnp.ones((KEYS, HD), BF)
        for b in range(2):
            place = place_of(b)
            for t in range(SPAN):
                kaug[b, t * TOK:(t + 1) * TOK, HD:] = elog[place + t]
            abias[b] = ((elog[place + 16].astype(F32) - 1.0) * BIG).astype(BF)

    def place_of(b):
        source = jnp.where(b == 0, 1 - y, y) * 2 * NZ + z * 2 + c
        return span_ref[source]

    for count, item in enumerate(PROLOGUE):
        if count == 4:
            tables()
        tick(item // 10, item % 10)
        if AHEAD + count < NSIG:
            kv_send(OWN_ORDER[AHEAD + count])
        if count in QUERIES_AT:
            q_send(QUERIES_AT.index(count))
    pltpu.make_async_copy(qbuf.at[1], qbuf.at[1], lq).wait()

    def scores(i):
        j, b = i // 2, i % 2
        place = place_of(b)
        for jj in range(HK):
            sig = 2 * jj

            @pl.when(j == jj)
            def _(sig=sig, jj=jj):
                @pl.when(b == 0)
                def _():
                    half = kvb[sig].at[pl.ds((1 - c) * 2 * NZ, 2 * NZ)]
                    remote(half, half, cs.at[sig], cr.at[sig], peer_c).wait_recv()
                    cols = pl.ds(jj * GROUP * HD, GROUP * HD)
                    part = qbuf.at[0, :, cols]
                    remote(part, part, yqs, yqr.at[jj], peer_y).wait_recv()

                for t in range(SPAN):
                    at = inv[jnp.maximum(place - 16 + t, 0)]
                    kaug[b, t * TOK:(t + 1) * TOK, :HD] = kvb[sig][at]

        for g in range(GROUP):
            cols = pl.ds(pl.multiple_of((j * GROUP + g) * HD, HD), HD)
            qa[g * TOK:(g + 1) * TOK, :HD] = qbuf[b, :, cols]
            qa[g * TOK:(g + 1) * TOK, HD:] = abias[b]
        s = lax.dot_general(qa[...], kaug[b], (((1,), (1,)), ((), ())), preferred_element_type=F32)
        causal = lax.broadcasted_iota(jnp.int32, (TOK, TOK), 1) <= lax.broadcasted_iota(jnp.int32, (TOK, TOK), 0)
        keep = b
        for g in range(GROUP):
            sg = s[g * TOK:(g + 1) * TOK]
            diag = jnp.where(causal, sg[:, KEYS - TOK:], -BIG)
            peak = diag
            for t in range(SPAN - 1):
                peak = jnp.maximum(peak, sg[:, t * TOK:(t + 1) * TOK])
            peak = jnp.max(peak, axis=1, keepdims=True) * SCALE
            pbuf[keep, g * TOK:(g + 1) * TOK, :KEYS - TOK] = jnp.exp2(sg[:, :KEYS - TOK] * SCALE - peak).astype(BF)
            pbuf[keep, g * TOK:(g + 1) * TOK, KEYS - TOK:] = jnp.exp2(diag * SCALE - peak).astype(BF)

    def values(i):
        j, b = i // 2, i % 2
        place = place_of(b)
        for jj in range(HK):
            sig = 2 * jj + 1

            @pl.when(j == jj)
            def _(sig=sig):
                @pl.when(b == 0)
                def _():
                    half = kvb[sig].at[pl.ds((1 - c) * 2 * NZ, 2 * NZ)]
                    remote(half, half, cs.at[sig], cr.at[sig], peer_c).wait_recv()

                for t in range(SPAN):
                    at = inv[jnp.maximum(place - 16 + t, 0)]
                    vaug[t * TOK:(t + 1) * TOK, :HD] = kvb[sig][at]

        o = lax.dot_general(pbuf[b], vaug[...], (((1,), (0,)), ((), ())), preferred_element_type=F32)
        o = (o[:, :HD] / o[:, HD:]).astype(BF)
        for g in range(GROUP):
            obuf[i, :, g * HD:(g + 1) * HD] = o[g * TOK:(g + 1) * TOK]
        cols = pl.ds(pl.multiple_of(j * GROUP * HD, GROUP * HD), GROUP * HD)

        @pl.when(b == 0)
        def _():
            for m, o_ref in enumerate((op_ref, or_ref)):
                @pl.when(y == m)
                def _(o_ref=o_ref):
                    remote(obuf.at[i], o_ref.at[:, cols], osend, orecv.at[j], peer_y).start()

        @pl.when(b == 1)
        def _():
            for m, o_ref in enumerate((op_ref, or_ref)):
                @pl.when(y == m)
                def _(o_ref=o_ref):
                    pltpu.make_async_copy(obuf.at[i], o_ref.at[:, cols], olocal.at[j]).start()

    @pl.loop(0, 4 * HK)
    def _(step):
        for k, items in BEFORE.items():
            @pl.when(step == k)
            def _(items=items):
                for item in items:
                    tick(item // 10, item % 10)

        i = step // 4 * 2 + step % 2

        @pl.when(step % 4 < 2)
        def _():
            scores(i)

        @pl.when(step % 4 >= 2)
        def _():
            values(i)

    for j in range(HK):
        part = obuf.at[j]
        remote(part, part, osend, orecv.at[j], peer_y).wait_recv()
        pltpu.make_async_copy(part, part, olocal.at[j]).wait()
    four = obuf.at[pl.ds(0, HK)]
    remote(four, four, osend, orecv.at[0], peer_y).wait_send()
    remote(qbuf.at[0], qbuf.at[0], yqs, yqr.at[0], peer_y).wait_send()
    eight = kvb[0].at[pl.ds(0, NSIG)]
    remote(eight, eight, ys, yr.at[0], peer_y).wait_send()
    for sig in range(NSIG):
        sent = kvb[sig].at[pl.ds(0, 14)]
        remote(sent, sent, zs.at[sig], zr.at[sig, 0, 0], up).wait_send()
        sent = kvb[sig].at[pl.ds(0, 16)]
        remote(sent, sent, cs.at[sig], cr.at[sig], peer_c).wait_send()


def on_device(n_ctx, q_policy, kv_policy, q_ref, kv_ref, doc_lengths, span_order):
    hbm = pl.BlockSpec(memory_space=pltpu.HBM)
    smem = pl.BlockSpec(memory_space=pltpu.SMEM)
    dma = pltpu.SemaphoreType.DMA
    out = pl.pallas_call(
        functools.partial(kernel, n_ctx),
        out_shape=[jax.ShapeDtypeStruct((TOK, HK * GROUP * HD), BF)] * 2,
        in_specs=[hbm] * 4 + [smem] * 2,
        out_specs=[hbm] * 2,
        scratch_shapes=[pltpu.VMEM((NBLK, TOK, HD), BF)] * NSIG
        + [
            pltpu.VMEM((2, TOK, HK * GROUP * HD), BF),
            pltpu.VMEM((2, KEYS, 2 * HD), BF),
            pltpu.VMEM((KEYS, 2 * HD), BF),
            pltpu.VMEM((2, ROWS, KEYS), BF),
            pltpu.VMEM((ROWS, 2 * HD), BF),
            pltpu.VMEM((2, TOK, HD), BF),
            pltpu.VMEM((NBLK + 16, TOK, HD), BF),
            pltpu.VMEM((2 * HK, TOK, GROUP * HD), BF),
            pltpu.SMEM((NBLK,), jnp.int32),
            dma((NSIG,)), dma, dma((NSIG,)), dma, dma((HK,)), dma,
            dma((NSIG, 4, 2)), dma((NSIG,)), dma((NSIG,)), dma((NSIG,)),
            dma((HK,)), dma, dma((HK,)),
        ],
        compiler_params=pltpu.CompilerParams(
            collective_id=0, has_side_effects=True, vmem_limit_bytes=63 * 2**20),
        cost_estimate=pl.CostEstimate(flops=6_000_000_000, bytes_accessed=4_000_000, transcendentals=12_000_000),
    )(q_policy, kv_policy, q_ref, kv_ref, doc_lengths, span_order)
    return tuple(out)


def solution(mesh):
    spec = P(("rep", "ctx"), None)
    return jax.shard_map(
        functools.partial(on_device, mesh.shape["ctx"]), mesh=mesh,
        in_specs=(spec, spec, spec, spec, P("rep"), P("rep")), out_specs=(spec, spec), check_vma=False)
```
